256 devices in a mesh: blk: 64 (over x, z, y_hi), head: 4 (over y_lo, core).
Axes of the slice: x: 4, y: 4 (y_hi: 2, y_lo: 2; y = y_hi * 2 + y_lo), z: 8, core: 2. Of those that a mesh axis runs over, the one named last changes fastest.
Arguments:
- queries: bfloat16 [32768, 1024], P('blk', 'head'), may hold values from -18 to 18, as said below
- key_rows: bfloat16 [32768, 128], P('blk'), may hold values from -18 to 18, as said below
- value_rows: bfloat16 [32768, 128], P('blk'), may hold values from -6 to 6
- grad_out: bfloat16 [32768, 1024], P('blk', 'head'), may hold values from -6 to 6
- positions: int32 [32768], replicated, may hold values from 0 to 32767, each once
Outputs:
- grad_queries: bfloat16 [32768, 1024], P('blk', 'head')
- grad_keys: bfloat16 [32768, 128], P(('blk', 'head'))
- grad_values: bfloat16 [32768, 128], P(('blk', 'head'))
The draws below stay inside these ranges and needn't reach their ends.
Inputs may be any that keep to these rules, and one draw needn't show every extreme that they name: `queries`: values of order one. `key_rows`: values of order one. `positions`: A permutation of 0 .. 32767.
All inputs are finite; a program needn't handle non-finite values.
Results may differ from the reference program's by a relative error of at most 0.0065.
Values may be sent and summed in bfloat16 or wider, within the bound.
No kernel may reach another device: no remote copies, remote signals or barrier semaphores. Data moves between devices by JAX's collectives and lax.ppermute only.
A program may use at most 64 MiB of HBM per device.

```python
import jax
import jax.numpy as jnp
from jax import lax

HD = 128
HEADS = 8
TOK_DEV = 512
SPAN = 4
TOKENS = 32768
N_BLK = 64


def drawn_rows(key):
    shared = jnp.clip(jax.random.normal(jax.random.fold_in(key, 101), (TOKENS, HD), jnp.float32), -4.0, 4.0)
    return shared


def draw_key_rows(key, part):
    shared = drawn_rows(key)
    return shared.astype(jnp.bfloat16)


def draw_queries(key, part):
    key = jax.random.fold_in(key, 8)
    return jnp.clip(jax.random.normal(key, (TOKENS, HEADS * HD), jnp.float32), -6.0, 6.0).astype(jnp.bfloat16)


def levels(key, dims, pieces, low, top_value):
    def one(dim, blocks):
        steps = jax.random.uniform(jax.random.fold_in(jax.random.fold_in(key, 6), dim), (blocks,), jnp.float32, low / len(pieces), top_value / len(pieces))
        return jnp.repeat(jnp.exp(steps), dims[dim] // blocks).reshape((-1,) + (1,) * (len(dims) - dim - 1))

    factor_of = one(*pieces[0])
    for cut in pieces[1:]:
        factor_of = factor_of * one(*cut)
    return factor_of


def centred(own_key, dims, width, most, cuts=(), kind=jnp.bfloat16):
    values = width * jax.random.normal(own_key, dims, jnp.float32)
    if cuts:
        values = values * levels(own_key, dims, cuts, -0.22, 0.18)
    return jnp.clip(values, -most, most).astype(kind)


def setup_inputs(seed: int = 0) -> dict:
    keys = jax.random.split(jax.random.key(seed), 6)
    queries = draw_queries(jax.random.fold_in(keys[5], 71), 0)
    key_rows = draw_key_rows(jax.random.fold_in(keys[5], 71), 0)
    value_rows = centred(keys[2], (TOKENS, HD), 1.0, 6.0, ((0, 64),))
    grad_out = centred(keys[3], (TOKENS, HEADS * HD), 1.0, 6.0, ((0, 64), (1, 4)))
    positions = jax.random.permutation(keys[4], TOKENS).astype(jnp.int32)
    return {"queries": queries, "key_rows": key_rows, "value_rows": value_rows, "grad_out": grad_out, "positions": positions}


def reference(queries, key_rows, value_rows, grad_out, positions):
    softmax_scale = 1.0 / (HD ** 0.5)
    query_blocks = queries.reshape(N_BLK, TOK_DEV, HEADS, HD).astype(jnp.float32)
    grad_blocks = grad_out.reshape(N_BLK, TOK_DEV, HEADS, HD).astype(jnp.float32)
    key_blocks = key_rows.reshape(N_BLK, TOK_DEV, HD).astype(jnp.float32)
    value_blocks = value_rows.reshape(N_BLK, TOK_DEV, HD).astype(jnp.float32)
    place_blocks = positions.reshape(N_BLK, TOK_DEV)

    def window_of(blocks, stripe):
        return jnp.concatenate([blocks[(stripe + offset) % N_BLK] for offset in range(SPAN)], axis=0)

    def visit(sums_pair, stripe):
        key_acc, value_acc = sums_pair
        query_here = query_blocks[stripe]
        grad_here = grad_blocks[stripe]
        key_window = window_of(key_blocks, stripe)
        value_window = window_of(value_blocks, stripe)
        place_window = window_of(place_blocks, stripe)
        allowed = place_window[None, :] <= place_blocks[stripe][:, None]
        scores = jnp.einsum("thd,kd->htk", query_here, key_window) * softmax_scale
        scores = jnp.where(allowed[None], scores, -jnp.inf)
        row_max = jnp.max(scores, axis=-1, keepdims=True)
        log_total = row_max + jnp.log(jnp.sum(jnp.exp(scores - row_max), axis=-1, keepdims=True))
        attention = jnp.exp(scores - log_total)
        attention_low = lax.optimization_barrier(attention.astype(jnp.bfloat16)).astype(jnp.float32)
        attended = jnp.einsum("htk,kd->thd", attention_low, value_window)
        delta_rows = jnp.sum(grad_here * attended, axis=-1).T
        grad_weights = jnp.einsum("thd,kd->htk", grad_here, value_window)
        grad_scores = attention * (grad_weights - delta_rows[:, :, None]) * softmax_scale
        grad_scores = lax.optimization_barrier(grad_scores.astype(jnp.bfloat16)).astype(jnp.float32)
        grad_query = jnp.einsum("htk,kd->thd", grad_scores, key_window)
        grad_key = jnp.einsum("htk,thd->kd", grad_scores, query_here)
        grad_value = jnp.einsum("htk,thd->kd", attention_low, grad_here)
        for offset in range(SPAN):
            target = (stripe + offset) % N_BLK
            key_acc = key_acc.at[target].add(grad_key[offset * TOK_DEV:(offset + 1) * TOK_DEV])
            value_acc = value_acc.at[target].add(grad_value[offset * TOK_DEV:(offset + 1) * TOK_DEV])
        return (key_acc, value_acc), grad_query.reshape(TOK_DEV, HEADS * HD).astype(jnp.bfloat16)

    empty = jnp.zeros((N_BLK, TOK_DEV, HD), jnp.float32)
    (key_acc, value_acc), query_grads = lax.scan(visit, (empty, empty), jnp.arange(N_BLK, dtype=jnp.int32))
    grad_queries = query_grads.reshape(TOKENS, HEADS * HD)
    grad_keys = key_acc.reshape(TOKENS, HD).astype(jnp.bfloat16)
    grad_values = value_acc.reshape(TOKENS, HD).astype(jnp.bfloat16)
    return (grad_queries, grad_keys, grad_values)
```

```python
import jax
import jax.numpy as jnp
from jax import lax
from jax.experimental import pallas as pl
from jax.experimental.pallas import tpu as pltpu
from jax.sharding import PartitionSpec as P

HD = 128
SPAN = 4
HEADS_CHIP = 4
NEG = -1e30
SCALE = 1.0 / HD**0.5
LOG2_SCALE = SCALE * 1.4426950408889634
F32 = jnp.float32
BF16 = jnp.bfloat16

NT = (((1,), (1,)), ((), ()))
NN = (((1,), (0,)), ((), ()))
TN = (((0,), (0,)), ((), ()))


def dot(a, b, dims):
    return lax.dot_general(a, b, dims, preferred_element_type=F32)


def call(body, outs, args, smem=0, flops=0, exps=0):
    specs = [pl.BlockSpec(memory_space=pltpu.SMEM)] * smem
    specs += [pl.BlockSpec(memory_space=pltpu.VMEM)] * (len(args) - smem)
    return pl.pallas_call(
        body,
        out_shape=outs,
        in_specs=specs,
        out_specs=[pl.BlockSpec(memory_space=pltpu.VMEM)] * len(outs),
        compiler_params=pltpu.CompilerParams(vmem_limit_bytes=40 * 1024 * 1024),
        cost_estimate=pl.CostEstimate(flops=flops, bytes_accessed=1 << 20, transcendentals=exps),
    )(*args)


def head_of(refs, head, first):
    ref = refs[head // 2]
    at = first + (head % 2) * HD
    return ref[:, at : at + HD]


def prepare(place, q_ref, g_ref, k_ref, v_ref, qg_ref, kv_ref):
    wide = q_ref.shape[1]
    qg_ref[:, :wide] = q_ref[...]
    qg_ref[:, wide:] = g_ref[...]
    core = place[1]
    for half in range(2):
        rows = pl.ds(pl.multiple_of(half * 256 + core * 128, 128), 128)
        kv_ref[half * 128 : (half + 1) * 128, :HD] = k_ref[rows, :]
        kv_ref[half * 128 : (half + 1) * 128, HD:] = v_ref[rows, :]


def scores_body(offset, place, pos_ref, kv_ref, qa_ref, qb_ref, *refs):
    prev_ref = refs[0] if offset else None
    p_ref, dp_ref, stats_ref = refs[-3:]
    rows = kv_ref.shape[0]
    toks = qa_ref.shape[0]
    key_row = place[2 + offset]
    query_row = place[0]
    columns = []
    for half in range(2):
        row = pos_ref[pl.ds(key_row + 2 * half, 1), :].astype(F32)
        columns.append(jnp.transpose(jnp.broadcast_to(row, (HD, HD))))
    key_pos = jnp.concatenate(columns, axis=0)
    biases = []
    for block in range(toks // HD):
        row = pos_ref[pl.ds(query_row + block, 1), :].astype(F32)
        biases.append(jnp.where(key_pos <= row, 0.0, NEG))
    bias = jnp.concatenate(biases, axis=1)
    keys = kv_ref[:, :HD]
    values = kv_ref[:, HD:]
    for head in range(HEADS_CHIP):
        cols = slice(head * toks, (head + 1) * toks)
        s = dot(keys, head_of((qa_ref, qb_ref), head, 0), NT) + bias
        dp = dot(values, head_of((qa_ref, qb_ref), head, 2 * HD), NT)
        top = jnp.max(s, axis=0, keepdims=True)
        if offset:
            before = prev_ref[0:1, cols]
            top = jnp.maximum(top, before)
        p = jnp.exp2((s - top) * LOG2_SCALE)
        total = jnp.sum(p, axis=0, keepdims=True)
        delta = jnp.sum(p * dp, axis=0, keepdims=True)
        if offset:
            fade = jnp.exp2((before - top) * LOG2_SCALE)
            total = total + prev_ref[1:2, cols] * fade
            delta = delta + prev_ref[2:3, cols] * fade
        p_ref[:, cols] = p
        dp_ref[:, cols] = dp
        stats_ref[0:1, cols] = top
        stats_ref[1:2, cols] = total
        stats_ref[2:3, cols] = delta


def grads_body(offset, first, last, *refs):
    p_ref, dp_ref, stats_ref, own_ref, mate_ref, kv_ref, qa_ref, qb_ref = refs[:8]
    refs = refs[8:]
    prev_ref = None
    if not first:
        prev_ref, refs = refs[0], refs[1:]
    dkv_ref, refs = refs[0], refs[1:]
    toks = qa_ref.shape[0]
    keys = kv_ref[:, :HD]
    dk = None
    for head in range(HEADS_CHIP):
        cols = slice(head * toks, (head + 1) * toks)
        other = (head + 2) % HEADS_CHIP
        across = slice(other * toks, (other + 1) * toks)
        top_own, top_mate = own_ref[0:1, cols], mate_ref[0:1, across]
        top = jnp.maximum(top_own, top_mate)
        fade_own = jnp.exp2((top_own - top) * LOG2_SCALE)
        fade_mate = jnp.exp2((top_mate - top) * LOG2_SCALE)
        total = own_ref[1:2, cols] * fade_own + mate_ref[1:2, across] * fade_mate
        delta = own_ref[2:3, cols] * fade_own + mate_ref[2:3, across] * fade_mate
        inverse = 1.0 / total
        delta = delta * inverse
        factor = jnp.exp2((stats_ref[0:1, cols] - top) * LOG2_SCALE) * inverse
        a = p_ref[:, cols] * factor
        ds = (a * (dp_ref[:, cols] - delta)).astype(BF16)
        dv_here = dot(a.astype(BF16), head_of((qa_ref, qb_ref), head, 2 * HD), NN)
        dk_here = dot(ds, head_of((qa_ref, qb_ref), head, 0), NN)
        dk = dk_here if dk is None else dk + dk_here
        dv = dv_here if head == 0 else dv + dv_here
        dq = dot(keys, ds, TN)
        if prev_ref is not None:
            dq = dq + prev_ref[head * HD : (head + 1) * HD, :]
        if last:
            out = refs[head // 2]
            at = (head % 2) * HD
            out[:, at : at + HD] = (jnp.transpose(dq) * SCALE).astype(out.dtype)
        else:
            refs[0][head * HD : (head + 1) * HD, :] = dq
    dkv_ref[:, :HD] = (dk * SCALE).astype(dkv_ref.dtype)
    dkv_ref[:, HD:] = dv.astype(dkv_ref.dtype)


def gather_body(place, own_ref, one_ref, two_ref, three_ref, mine_ref, theirs_ref):
    chip = place[6]

    def summed(half):
        rows = pl.ds(pl.multiple_of(half * 128, 128), 128)
        near = own_ref[rows, :] + one_ref[rows, :].astype(F32)
        return near + two_ref[rows, :].astype(F32) + three_ref[rows, :].astype(F32)

    mine_ref[...] = summed(chip)
    theirs_ref[...] = summed(1 - chip).astype(BF16)


def finish_body(mine_ref, got_ref, dq_own_ref, dq_got_ref, dq_ref, dk_ref, dv_ref):
    total = mine_ref[...] + got_ref[...].astype(F32)
    dk_ref[...] = total[:, :HD].astype(BF16)
    dv_ref[...] = total[:, HD:].astype(BF16)
    dq_ref[...] = (dq_own_ref[...] + dq_got_ref[...].astype(F32)).astype(BF16)


def shards(queries, key_rows, value_rows, grad_out, positions):
    toks, wide = queries.shape
    stripes = lax.axis_size("blk")
    heads = lax.axis_size("head")
    here = lax.axis_index("blk")
    head = lax.axis_index("head")
    core, chip = head % 2, head // 2
    step = toks // HD
    place = jnp.stack(
        [here * step, core]
        + [(here + k) % stripes * step + core for k in range(SPAN)]
        + [chip, core]
    ).astype(jnp.int32)
    pos = positions.reshape(-1, HD)

    def route(value, offset):
        flip = 2 if offset % 2 else 0
        pairs = [
            (s * heads + h, (s + offset) % stripes * heads + (h ^ flip))
            for s in range(stripes)
            for h in range(heads)
        ]
        return lax.ppermute(value, ("blk", "head"), pairs)

    def swap(value, bit):
        return lax.ppermute(value, "head", [(h, h ^ bit) for h in range(heads)])

    def vmem(shape, dtype):
        return pltpu.VMEM(shape, dtype)

    half = toks // 2
    lanes = HEADS_CHIP * toks
    qg, kv = call(
        prepare,
        [vmem((toks, 2 * wide), BF16), vmem((half, 2 * HD), BF16)],
        (place, queries, grad_out, key_rows, value_rows),
        smem=1,
    )
    qg_mate = swap(qg, 1)
    window = [kv] + [route(kv, -k) for k in range(1, SPAN)]
    kept = []
    stats = None
    flops = 2 * 2 * HD * half * lanes
    for k in range(SPAN):
        args = (place, pos, window[k], qg, qg_mate) + ((stats,) if k else ())
        p, dp, stats = call(
            lambda *refs, k=k: scores_body(k, *refs),
            [vmem((half, lanes), F32), vmem((half, lanes), F32), vmem((8, lanes), F32)],
            args,
            smem=1,
            flops=flops,
            exps=half * lanes,
        )
        kept.append((p, dp, stats))
    stats_mate = swap(stats, 1)
    sent = []
    dq = None
    for k in reversed(range(SPAN)):
        p, dp, own = kept[k]
        args = (p, dp, own, stats, stats_mate, window[k], qg, qg_mate)
        outs = [vmem((half, 2 * HD), BF16 if k else F32)]
        if k:
            outs += [vmem((HEADS_CHIP * HD, toks), F32)]
        else:
            outs += [vmem((toks, wide), F32), vmem((toks, wide), BF16)]
        got = call(
            lambda *refs, k=k: grads_body(k, k == SPAN - 1, k == 0, *refs),
            outs,
            args if dq is None else args + (dq,),
            flops=flops * 3 // 2,
        )
        dq = got[1]
        sent.append(route(got[0], k) if k else got[0])
    dq_own, dq_far = got[1:]
    dq_got = swap(dq_far, 1)
    mine, theirs = call(
        gather_body,
        [vmem((half // 2, 2 * HD), F32), vmem((half // 2, 2 * HD), BF16)],
        (place, sent[3], sent[2], sent[1], sent[0]),
        smem=1,
    )
    got = swap(theirs, 2)
    return tuple(
        call(
            finish_body,
            [
                jax.ShapeDtypeStruct((toks, wide), BF16),
                jax.ShapeDtypeStruct((half // 2, HD), BF16),
                jax.ShapeDtypeStruct((half // 2, HD), BF16),
            ],
            (mine, got, dq_own, dq_got),
        )
    )


def solution(mesh):
    return jax.shard_map(
        shards,
        mesh=mesh,
        in_specs=(P("blk", "head"), P("blk", None), P("blk", None), P("blk", "head"), P()),
        out_specs=(P("blk", "head"), P(("blk", "head"), None), P(("blk", "head"), None)),
        check_vma=False,
    )
```

```python
import jax
import jax.numpy as jnp
from jax import lax
from jax.experimental import pallas as pl
from jax.experimental.pallas import tpu as pltpu
from jax.sharding import PartitionSpec as P

HD = 128
SPAN = 4
HEADS_CHIP = 4
NEG = -1e30
SCALE = 1.0 / HD**0.5
LOG2_SCALE = SCALE * 1.4426950408889634
F32 = jnp.float32
BF16 = jnp.bfloat16

NT = (((1,), (1,)), ((), ()))
NN = (((1,), (0,)), ((), ()))
TN = (((0,), (0,)), ((), ()))


def dot(a, b, dims):
    return lax.dot_general(a, b, dims, preferred_element_type=F32)


def call(body, outs, args, flops=0, exps=0):
    whole = pl.BlockSpec(memory_space=pltpu.VMEM)
    return pl.pallas_call(
        body,
        out_shape=outs,
        in_specs=[whole] * len(args),
        out_specs=[whole] * len(outs),
        compiler_params=pltpu.CompilerParams(vmem_limit_bytes=16 * 1024 * 1024),
        cost_estimate=pl.CostEstimate(flops=flops, bytes_accessed=1 << 20, transcendentals=exps),
    )(*args)


def head_of(refs, head, first):
    ref = refs[head // 2]
    at = first + (head % 2) * HD
    return ref[:, at : at + HD]


def prepare(q_hbm, g_hbm, k_hbm, v_hbm, pos_hbm, qg_ref, kv_ref, pos_ref, sems):
    wide = q_hbm.shape[1]
    core = lax.axis_index("head") % 2
    block = lax.axis_index("blk") * (q_hbm.shape[0] // HD) // 8
    blocks = pos_hbm.shape[0] // 8
    copies = []
    for half in range(2):
        source = pl.ds(pl.multiple_of(half * 256 + core * 128, 128), 128)
        target = pl.ds(half * 128, 128)
        copies.append((k_hbm.at[source, :], kv_ref.at[target, pl.ds(0, HD)]))
        copies.append((v_hbm.at[source, :], kv_ref.at[target, pl.ds(HD, HD)]))
    copies.append((q_hbm, qg_ref.at[:, pl.ds(0, wide)]))
    copies.append((g_hbm, qg_ref.at[:, pl.ds(wide, wide)]))
    for i in range(3):
        row = pl.multiple_of((block + i) % blocks * 8, 8)
        copies.append((pos_hbm.at[pl.ds(row, 8), :], pos_ref.at[pl.ds(i * 8, 8), :]))
    copies = [
        pltpu.make_async_copy(source, target, sems.at[i])
        for i, (source, target) in enumerate(copies)
    ]
    for copy in copies:
        copy.start()
    for copy in copies:
        copy.wait()


def mask_body(pos_ref, bias_ref, flag_ref):
    core = lax.axis_index("head") % 2
    chip = lax.axis_index("head") // 2
    toks = bias_ref.shape[1]
    query_row = lax.axis_index("blk") * (toks // HD) % 8
    queries = [
        pos_ref[pl.ds(query_row + i, 1), :].astype(F32) for i in range(toks // HD)
    ]
    for k in range(SPAN):
        for half in range(2):
            row = pos_ref[pl.ds(query_row + k * (toks // HD) + 2 * half + core, 1), :]
            keys = jnp.transpose(jnp.broadcast_to(row.astype(F32), (HD, HD)))
            rows = slice((2 * k + half) * HD, (2 * k + half + 1) * HD)
            for i, query in enumerate(queries):
                bias_ref[rows, i * HD : (i + 1) * HD] = jnp.where(keys <= query, 0.0, NEG)
    flag_ref[...] = jnp.full(flag_ref.shape, chip, F32)


def scores_body(offset, bias_ref, kv_ref, qa_ref, qb_ref, *refs):
    prev_ref = refs[0] if len(refs) == 4 else None
    p_ref, dp_ref, stats_ref = refs[-3:]
    rows = kv_ref.shape[0]
    toks = qa_ref.shape[0]
    bias = bias_ref[offset * rows : (offset + 1) * rows, :]
    keys = kv_ref[:, :HD]
    values = kv_ref[:, HD:]
    for head in range(HEADS_CHIP):
        cols = slice(head * toks, (head + 1) * toks)
        s = dot(keys, head_of((qa_ref, qb_ref), head, 0), NT) + bias
        dp = dot(values, head_of((qa_ref, qb_ref), head, 2 * HD), NT)
        top = jnp.max(s, axis=0, keepdims=True)
        if prev_ref is not None:
            before = prev_ref[0:1, cols]
            top = jnp.maximum(top, before)
        p = jnp.exp2((s - top) * LOG2_SCALE)
        total = jnp.sum(p, axis=0, keepdims=True)
        delta = jnp.sum(p * dp, axis=0, keepdims=True)
        if prev_ref is not None:
            fade = jnp.exp2((before - top) * LOG2_SCALE)
            total = total + prev_ref[1:2, cols] * fade
            delta = delta + prev_ref[2:3, cols] * fade
        p_ref[:, cols] = p
        dp_ref[:, cols] = dp
        stats_ref[0:1, cols] = top
        stats_ref[1:2, cols] = total
        stats_ref[2:3, cols] = delta


def grads_body(flip, flag_ref, p_ref, dp_ref, stats_ref, own_ref, mate_ref, qa_ref, qb_ref, *outs):
    ds_ref, keep_ref, give_ref = outs
    toks = qa_ref.shape[0]
    for head in range(HEADS_CHIP):
        cols = slice(head * toks, (head + 1) * toks)
        other = (head + 2) % HEADS_CHIP
        across = slice(other * toks, (other + 1) * toks)
        top_own, top_mate = own_ref[0:1, cols], mate_ref[0:1, across]
        top = jnp.maximum(top_own, top_mate)
        fade_own = jnp.exp2((top_own - top) * LOG2_SCALE)
        fade_mate = jnp.exp2((top_mate - top) * LOG2_SCALE)
        total = own_ref[1:2, cols] * fade_own + mate_ref[1:2, across] * fade_mate
        delta = own_ref[2:3, cols] * fade_own + mate_ref[2:3, across] * fade_mate
        inverse = 1.0 / total
        delta = delta * inverse
        factor = jnp.exp2((stats_ref[0:1, cols] - top) * LOG2_SCALE) * inverse
        a = p_ref[:, cols] * factor
        ds = (a * (dp_ref[:, cols] - delta)).astype(BF16)
        ds_ref[:, cols] = ds
        dv_here = dot(a.astype(BF16), head_of((qa_ref, qb_ref), head, 2 * HD), NN)
        dk_here = dot(ds, head_of((qa_ref, qb_ref), head, 0), NN)
        dk = dk_here if head == 0 else dk + dk_here
        dv = dv_here if head == 0 else dv + dv_here
    both = jnp.concatenate([dk * SCALE, dv], axis=1)
    half = both.shape[0] // 2
    first, second = (both[half:], both[:half]) if flip else (both[:half], both[half:])
    upper = flag_ref[0:1, :] > 0
    upper = jnp.concatenate([upper, upper], axis=1)
    keep_ref[...] = jnp.where(upper, second, first)
    give_ref[...] = jnp.where(upper, first, second).astype(BF16)


def query_body(heads, ds_refs, kv_refs, out_ref):
    toks = out_ref.shape[0]
    for i, head in enumerate(heads):
        dq = None
        for ds_ref, kv_ref in zip(ds_refs, kv_refs):
            here = dot(kv_ref[:, :HD], ds_ref[:, head * toks : (head + 1) * toks], TN)
            dq = here if dq is None else dq + here
        out_ref[:, i * HD : (i + 1) * HD] = (jnp.transpose(dq) * SCALE).astype(out_ref.dtype)


def finish_body(mine_ref, got_ref, one_ref, two_ref, three_ref, dk_ref, dv_ref):
    total = mine_ref[...] + got_ref[...].astype(F32) + one_ref[...].astype(F32)
    total = total + two_ref[...].astype(F32) + three_ref[...].astype(F32)
    dk_ref[...] = total[:, :HD].astype(BF16)
    dv_ref[...] = total[:, HD:].astype(BF16)


def query_sum_body(own_ref, got_ref, dq_ref):
    dq_ref[...] = (own_ref[...] + got_ref[...].astype(F32)).astype(BF16)


def shards(queries, key_rows, value_rows, grad_out, positions):
    toks, wide = queries.shape
    stripes = lax.axis_size("blk")
    heads = lax.axis_size("head")
    pos = positions.reshape(-1, HD)

    def route(value, offset):
        flip = 2 if offset % 2 else 0
        pairs = [
            (s * heads + h, (s + offset) % stripes * heads + (h ^ flip))
            for s in range(stripes)
            for h in range(heads)
        ]
        return lax.ppermute(value, ("blk", "head"), pairs)

    def swap(value, bit):
        return lax.ppermute(value, "head", [(h, h ^ bit) for h in range(heads)])

    def vmem(shape, dtype):
        return pltpu.VMEM(shape, dtype)

    half = toks // 2
    lanes = HEADS_CHIP * toks
    hbm = pl.BlockSpec(memory_space=pltpu.HBM)
    whole = pl.BlockSpec(memory_space=pltpu.VMEM)
    qg, kv, pos = pl.pallas_call(
        prepare,
        out_shape=[
            vmem((toks, 2 * wide), BF16),
            vmem((half, 2 * HD), BF16),
            vmem((24, HD), jnp.int32),
        ],
        in_specs=[hbm] * 5,
        out_specs=[whole] * 3,
        scratch_shapes=[pltpu.SemaphoreType.DMA((9,))],
        compiler_params=pltpu.CompilerParams(vmem_limit_bytes=16 * 1024 * 1024),
    )(*(pltpu.with_memory_space_constraint(v, pltpu.HBM) for v in (queries, grad_out, key_rows, value_rows, pos)))
    qg_mate = swap(qg, 1)
    bias, flag = call(mask_body, [vmem((SPAN * half, toks), F32), vmem((8, HD), F32)], (pos,))
    window = {0: kv}
    for k in (2, 1, 3):
        window[k] = route(kv, -k)
    kept = {}
    stats = None
    flops = 2 * 2 * HD * half * lanes
    for k in (0, 2, 1, 3):
        args = (bias, window[k], qg, qg_mate) + (() if stats is None else (stats,))
        p, dp, stats = call(
            lambda *refs, k=k: scores_body(k, *refs),
            [vmem((half, lanes), F32), vmem((half, lanes), F32), vmem((8, lanes), F32)],
            args,
            flops=flops,
            exps=half * lanes,
        )
        kept[k] = (p, dp, stats)
    stats_mate = swap(stats, 1)
    grads = {}
    for k in (3, 2, 1, 0):
        p, dp, own = kept[k]

        grads[k] = call(
            lambda *refs, k=k: grads_body(k % 2, *refs),
            [
                vmem((half, lanes), BF16),
                vmem((half // 2, 2 * HD), F32),
                vmem((half // 2, 2 * HD), BF16),
            ],
            (flag, p, dp, own, stats, stats_mate, qg, qg_mate),
            flops=flops,
        )
    pushed = {}
    for k in (3, 2, 1, 0):
        _, keep, give = grads[k]
        got = swap(give, 2)
        pushed[k] = (keep, got)
        if k:
            pushed[k] = route((keep + got.astype(F32)).astype(BF16), k)

    def query_part(heads, kind):
        def body(*refs):
            query_body(heads, refs[:SPAN], refs[SPAN : 2 * SPAN], refs[2 * SPAN])

        args = [grads[k][0] for k in range(SPAN)] + [window[k] for k in range(SPAN)]
        return call(body, [vmem((toks, wide), kind)], args, flops=flops)[0]

    dq_got = swap(query_part((2, 3), BF16), 1)
    dq_own = query_part((0, 1), F32)
    [dq] = call(query_sum_body, [jax.ShapeDtypeStruct((toks, wide), BF16)], (dq_own, dq_got))
    dk, dv = call(
        finish_body,
        [jax.ShapeDtypeStruct((half // 2, HD), BF16)] * 2,
        (*pushed[0], pushed[1], pushed[2], pushed[3]),
    )
    return dq, dk, dv


def solution(mesh):
    return jax.shard_map(
        shards,
        mesh=mesh,
        in_specs=(P("blk", "head"), P("blk", None), P("blk", None), P("blk", "head"), P()),
        out_specs=(P("blk", "head"), P(("blk", "head"), None), P(("blk", "head"), None)),
        check_vma=False,
    )
```

```python
import jax
import jax.numpy as jnp
from jax import lax
from jax.experimental import pallas as pl
from jax.experimental.pallas import tpu as pltpu
from jax.sharding import PartitionSpec as P

HD = 128
SPAN = 4
HEADS_CHIP = 4
NEG = -1e30
SCALE = 1.0 / HD**0.5
LOG2_SCALE = SCALE * 1.4426950408889634
F32 = jnp.float32
BF16 = jnp.bfloat16

NT = (((1,), (1,)), ((), ()))
NN = (((1,), (0,)), ((), ()))
TN = (((0,), (0,)), ((), ()))


def dot(a, b, dims):
    return lax.dot_general(a, b, dims, preferred_element_type=F32)


def call(body, outs, args, flops=0, exps=0):
    whole = pl.BlockSpec(memory_space=pltpu.VMEM)
    return pl.pallas_call(
        body,
        out_shape=outs,
        in_specs=[whole] * len(args),
        out_specs=[whole] * len(outs),
        compiler_params=pltpu.CompilerParams(vmem_limit_bytes=16 * 1024 * 1024),
        cost_estimate=pl.CostEstimate(flops=flops, bytes_accessed=1 << 20, transcendentals=exps),
    )(*args)


def head_of(refs, head, first):
    ref = refs[head // 2]
    at = first + (head % 2) * HD
    return ref[:, at : at + HD]


def prepare(q_hbm, g_hbm, k_hbm, v_hbm, pos_hbm, qg_ref, kv_ref, pos_ref, sems):
    wide = q_hbm.shape[1]
    core = lax.axis_index("head") % 2
    block = lax.axis_index("blk") * (q_hbm.shape[0] // HD) // 8
    blocks = pos_hbm.shape[0] // 8
    copies = []
    for half in range(2):
        source = pl.ds(pl.multiple_of(half * 256 + core * 128, 128), 128)
        target = pl.ds(half * 128, 128)
        copies.append((k_hbm.at[source, :], kv_ref.at[target, pl.ds(0, HD)]))
        copies.append((v_hbm.at[source, :], kv_ref.at[target, pl.ds(HD, HD)]))
    copies.append((q_hbm, qg_ref.at[:, pl.ds(0, wide)]))
    copies.append((g_hbm, qg_ref.at[:, pl.ds(wide, wide)]))
    for i in range(3):
        row = pl.multiple_of((block + i) % blocks * 8, 8)
        copies.append((pos_hbm.at[pl.ds(row, 8), :], pos_ref.at[pl.ds(i * 8, 8), :]))
    copies = [
        pltpu.make_async_copy(source, target, sems.at[i])
        for i, (source, target) in enumerate(copies)
    ]
    for copy in copies:
        copy.start()
    for copy in copies:
        copy.wait()


def mask_body(pos_ref, bias_ref, flag_ref):
    core = lax.axis_index("head") % 2
    chip = lax.axis_index("head") // 2
    toks = bias_ref.shape[1]
    query_row = lax.axis_index("blk") * (toks // HD) % 8
    queries = [
        pos_ref[pl.ds(query_row + i, 1), :].astype(F32) for i in range(toks // HD)
    ]
    for k in range(SPAN):
        for half in range(2):
            row = pos_ref[pl.ds(query_row + k * (toks // HD) + 2 * half + core, 1), :]
            keys = jnp.transpose(jnp.broadcast_to(row.astype(F32), (HD, HD)))
            rows = slice((2 * k + half) * HD, (2 * k + half + 1) * HD)
            for i, query in enumerate(queries):
                bias_ref[rows, i * HD : (i + 1) * HD] = jnp.where(keys <= query, 0.0, NEG)
    flag_ref[...] = jnp.full(flag_ref.shape, chip, F32)


def scores_body(offset, bias_ref, kv_ref, qa_ref, qb_ref, *refs):
    prev_ref = refs[0] if len(refs) == 4 else None
    p_ref, dp_ref, stats_ref = refs[-3:]
    rows = kv_ref.shape[0]
    toks = qa_ref.shape[0]
    bias = bias_ref[offset * rows : (offset + 1) * rows, :]
    keys = kv_ref[:, :HD]
    values = kv_ref[:, HD:]
    for head in range(HEADS_CHIP):
        cols = slice(head * toks, (head + 1) * toks)
        s = dot(keys, head_of((qa_ref, qb_ref), head, 0), NT) + bias
        dp = dot(values, head_of((qa_ref, qb_ref), head, 2 * HD), NT)
        top = jnp.max(s, axis=0, keepdims=True)
        if prev_ref is not None:
            before = prev_ref[0:1, cols]
            top = jnp.maximum(top, before)
        p = jnp.exp2((s - top) * LOG2_SCALE)
        total = jnp.sum(p, axis=0, keepdims=True)
        delta = jnp.sum(p * dp, axis=0, keepdims=True)
        if prev_ref is not None:
            fade = jnp.exp2((before - top) * LOG2_SCALE)
            total = total + prev_ref[1:2, cols] * fade
            delta = delta + prev_ref[2:3, cols] * fade
        p_ref[:, cols] = p
        dp_ref[:, cols] = dp
        stats_ref[0:1, cols] = top
        stats_ref[1:2, cols] = total
        stats_ref[2:3, cols] = delta


def grads_body(flips, flag_ref, own_ref, mate_ref, qa_ref, qb_ref, *refs):
    pairs = len(flips)
    kept, refs = refs[: 3 * pairs], refs[3 * pairs :]
    ds_refs, keep_refs, give_ref = refs[:pairs], refs[pairs : 2 * pairs], refs[2 * pairs]
    toks = qa_ref.shape[0]
    sums = [None] * pairs
    for head in range(HEADS_CHIP):
        cols = slice(head * toks, (head + 1) * toks)
        other = (head + 2) % HEADS_CHIP
        across = slice(other * toks, (other + 1) * toks)
        top_own, top_mate = own_ref[0:1, cols], mate_ref[0:1, across]
        top = jnp.maximum(top_own, top_mate)
        fade_own = jnp.exp2((top_own - top) * LOG2_SCALE)
        fade_mate = jnp.exp2((top_mate - top) * LOG2_SCALE)
        total = own_ref[1:2, cols] * fade_own + mate_ref[1:2, across] * fade_mate
        delta = own_ref[2:3, cols] * fade_own + mate_ref[2:3, across] * fade_mate
        inverse = 1.0 / total
        delta = delta * inverse
        for i in range(pairs):
            p_ref, dp_ref, stats_ref = kept[3 * i : 3 * i + 3]
            factor = jnp.exp2((stats_ref[0:1, cols] - top) * LOG2_SCALE) * inverse
            a = p_ref[:, cols] * factor
            ds = (a * (dp_ref[:, cols] - delta)).astype(BF16)
            ds_refs[i][:, cols] = ds
            dv = dot(a.astype(BF16), head_of((qa_ref, qb_ref), head, 2 * HD), NN)
            dk = dot(ds, head_of((qa_ref, qb_ref), head, 0), NN)
            if sums[i] is None:
                sums[i] = (dk, dv)
            else:
                sums[i] = (sums[i][0] + dk, sums[i][1] + dv)
    upper = flag_ref[0:1, :] > 0
    upper = jnp.concatenate([upper, upper], axis=1)
    for i, flip in enumerate(flips):
        both = jnp.concatenate([sums[i][0] * SCALE, sums[i][1]], axis=1)
        half = both.shape[0] // 2
        first, second = (both[half:], both[:half]) if flip else (both[:half], both[half:])
        keep_refs[i][...] = jnp.where(upper, second, first)
        give_ref[i * half : (i + 1) * half, :] = jnp.where(upper, first, second).astype(BF16)


def query_body(heads, ds_refs, kv_refs, out_ref):
    toks = out_ref.shape[0]
    for i, head in enumerate(heads):
        dq = None
        for ds_ref, kv_ref in zip(ds_refs, kv_refs):
            here = dot(kv_ref[:, :HD], ds_ref[:, head * toks : (head + 1) * toks], TN)
            dq = here if dq is None else dq + here
        out_ref[:, i * HD : (i + 1) * HD] = (jnp.transpose(dq) * SCALE).astype(out_ref.dtype)


def finish_body(mine_ref, got_ref, one_ref, two_ref, three_ref, dq_own_ref, dq_got_ref, *outs):
    dq_ref, dk_ref, dv_ref = outs
    dq_ref[...] = (dq_own_ref[...] + dq_got_ref[...].astype(F32)).astype(BF16)
    rows = mine_ref.shape[0]
    total = mine_ref[...] + got_ref[rows:, :].astype(F32) + one_ref[...].astype(F32)
    total = total + two_ref[...].astype(F32) + three_ref[...].astype(F32)
    dk_ref[...] = total[:, :HD].astype(BF16)
    dv_ref[...] = total[:, HD:].astype(BF16)


def shards(queries, key_rows, value_rows, grad_out, positions):
    toks, wide = queries.shape
    stripes = lax.axis_size("blk")
    heads = lax.axis_size("head")
    pos = positions.reshape(-1, HD)

    def route(value, offset):
        flip = 2 if offset % 2 else 0
        pairs = [
            (s * heads + h, (s + offset) % stripes * heads + (h ^ flip))
            for s in range(stripes)
            for h in range(heads)
        ]
        return lax.ppermute(value, ("blk", "head"), pairs)

    def swap(value, bit):
        return lax.ppermute(value, "head", [(h, h ^ bit) for h in range(heads)])

    def vmem(shape, dtype):
        return pltpu.VMEM(shape, dtype)

    half = toks // 2
    lanes = HEADS_CHIP * toks
    hbm = pl.BlockSpec(memory_space=pltpu.HBM)
    whole = pl.BlockSpec(memory_space=pltpu.VMEM)
    qg, kv, pos = pl.pallas_call(
        prepare,
        out_shape=[
            vmem((toks, 2 * wide), BF16),
            vmem((half, 2 * HD), BF16),
            vmem((24, HD), jnp.int32),
        ],
        in_specs=[hbm] * 5,
        out_specs=[whole] * 3,
        scratch_shapes=[pltpu.SemaphoreType.DMA((9,))],
        compiler_params=pltpu.CompilerParams(vmem_limit_bytes=16 * 1024 * 1024),
    )(*(pltpu.with_memory_space_constraint(v, pltpu.HBM) for v in (queries, grad_out, key_rows, value_rows, pos)))
    qg_mate = swap(qg, 1)
    bias, flag = call(mask_body, [vmem((SPAN * half, toks), F32), vmem((8, HD), F32)], (pos,))
    window = {0: kv}
    for k in (2, 1, 3):
        window[k] = route(kv, -k)
    kept = {}
    stats = None
    flops = 2 * 2 * HD * half * lanes
    for k in (0, 2, 1, 3):
        args = (bias, window[k], qg, qg_mate) + (() if stats is None else (stats,))
        p, dp, stats = call(
            lambda *refs, k=k: scores_body(k, *refs),
            [vmem((half, lanes), F32), vmem((half, lanes), F32), vmem((8, lanes), F32)],
            args,
            flops=flops,
            exps=half * lanes,
        )
        kept[k] = (p, dp, stats)
    stats_mate = swap(stats, 1)
    ds = {}
    pushed = {}
    for pair in ((2, 1), (3, 0)):
        outs = call(
            lambda *refs, pair=pair: grads_body([k % 2 for k in pair], *refs),
            [vmem((half, lanes), BF16)] * 2
            + [vmem((half // 2, 2 * HD), F32)] * 2
            + [vmem((half, 2 * HD), BF16)],
            (flag, stats, stats_mate, qg, qg_mate, *kept[pair[0]], *kept[pair[1]]),
            flops=2 * flops,
        )
        ds[pair[0]], ds[pair[1]] = outs[:2]
        keep, give = outs[2:4], outs[4]
        got = swap(give, 2)
        for i, k in enumerate(pair):
            if k:
                here = got[i * half // 2 : (i + 1) * half // 2].astype(F32)
                pushed[k] = route((keep[i] + here).astype(BF16), k)
            else:
                mine, mine_got = keep[i], got

    def query_part(heads, kind):
        def body(*refs):
            query_body(heads, refs[:SPAN], refs[SPAN : 2 * SPAN], refs[2 * SPAN])

        args = [ds[k] for k in range(SPAN)] + [window[k] for k in range(SPAN)]
        return call(body, [vmem((toks, wide), kind)], args, flops=flops)[0]

    dq_got = swap(query_part((2, 3), BF16), 1)
    dq_own = query_part((0, 1), F32)
    return tuple(
        call(
            finish_body,
            [jax.ShapeDtypeStruct((toks, wide), BF16)]
            + [jax.ShapeDtypeStruct((half // 2, HD), BF16)] * 2,
            (mine, mine_got, *(pushed[k] for k in (1, 2, 3)), dq_own, dq_got),
        )
    )


def solution(mesh):
    return jax.shard_map(
        shards,
        mesh=mesh,
        in_specs=(P("blk", "head"), P("blk", None), P("blk", None), P("blk", "head"), P()),
        out_specs=(P("blk", "head"), P(("blk", "head"), None), P(("blk", "head"), None)),
        check_vma=False,
    )
```

```python
import jax
import jax.numpy as jnp
from jax import lax
from jax.experimental import pallas as pl
from jax.experimental.pallas import tpu as pltpu
from jax.sharding import PartitionSpec as P

HD = 128
SPAN = 4
HEADS_CHIP = 4
NEG = -1e30
SCALE = 1.0 / HD**0.5
LOG2_SCALE = SCALE * 1.4426950408889634
F32 = jnp.float32
BF16 = jnp.bfloat16

NT = (((1,), (1,)), ((), ()))
NN = (((1,), (0,)), ((), ()))
TN = (((0,), (0,)), ((), ()))


def dot(a, b, dims):
    return lax.dot_general(a, b, dims, preferred_element_type=F32)


def call(body, outs, args, flops=0, exps=0):
    whole = pl.BlockSpec(memory_space=pltpu.VMEM)
    return pl.pallas_call(
        body,
        out_shape=outs,
        in_specs=[whole] * len(args),
        out_specs=[whole] * len(outs),
        compiler_params=pltpu.CompilerParams(vmem_limit_bytes=16 * 1024 * 1024),
        cost_estimate=pl.CostEstimate(flops=flops, bytes_accessed=1 << 20, transcendentals=exps),
    )(*args)


def head_of(refs, head, first):
    ref = refs[head // 2]
    at = first + (head % 2) * HD
    return ref[:, at : at + HD]


def prepare(q_hbm, g_hbm, k_hbm, v_hbm, pos_hbm, qg_ref, kv_ref, pos_ref, sems):
    wide = q_hbm.shape[1]
    core = lax.axis_index("head") % 2
    chip = lax.axis_index("head") // 2
    block = lax.axis_index("blk") * (q_hbm.shape[0] // HD) // 8
    blocks = pos_hbm.shape[0] // 8
    copies = []
    for half in range(2):
        source = pl.ds(pl.multiple_of((chip ^ half) * 256 + core * 128, 128), 128)
        target = pl.ds(half * 128, 128)
        copies.append((k_hbm.at[source, :], kv_ref.at[target, pl.ds(0, HD)]))
        copies.append((v_hbm.at[source, :], kv_ref.at[target, pl.ds(HD, HD)]))
    copies.append((q_hbm, qg_ref.at[:, pl.ds(0, wide)]))
    copies.append((g_hbm, qg_ref.at[:, pl.ds(wide, wide)]))
    for i in range(3):
        row = pl.multiple_of((block + i) % blocks * 8, 8)
        copies.append((pos_hbm.at[pl.ds(row, 8), :], pos_ref.at[pl.ds(i * 8, 8), :]))
    copies = [
        pltpu.make_async_copy(source, target, sems.at[i])
        for i, (source, target) in enumerate(copies)
    ]
    for copy in copies:
        copy.start()
    for copy in copies:
        copy.wait()


def mask_body(pos_ref, bias_ref):
    core = lax.axis_index("head") % 2
    chip = lax.axis_index("head") // 2
    toks = bias_ref.shape[1]
    query_row = lax.axis_index("blk") * (toks // HD) % 8
    queries = [
        pos_ref[pl.ds(query_row + i, 1), :].astype(F32) for i in range(toks // HD)
    ]
    for k in range(SPAN):
        for half in range(2):
            place = query_row + k * (toks // HD) + 2 * (chip ^ (k + half) % 2) + core
            row = pos_ref[pl.ds(place, 1), :]
            keys = jnp.transpose(jnp.broadcast_to(row.astype(F32), (HD, HD)))
            rows = slice((2 * k + half) * HD, (2 * k + half + 1) * HD)
            for i, query in enumerate(queries):
                bias_ref[rows, i * HD : (i + 1) * HD] = jnp.where(keys <= query, 0.0, NEG)


def joined(refs):
    return refs[0][...] if len(refs) == 1 else jnp.concatenate([r[...] for r in refs], axis=0)


def scores_body(offset, parts, bias_ref, qa_ref, qb_ref, *refs):
    kv, refs = joined(refs[:parts]), refs[parts:]
    prev_ref = refs[0] if len(refs) == 4 else None
    p_ref, dp_ref, stats_ref = refs[-3:]
    rows = kv.shape[0]
    toks = qa_ref.shape[0]
    bias = bias_ref[offset * rows : (offset + 1) * rows, :]
    keys = kv[:, :HD]
    values = kv[:, HD:]
    for head in range(HEADS_CHIP):
        cols = slice(head * toks, (head + 1) * toks)
        s = dot(keys, head_of((qa_ref, qb_ref), head, 0), NT) + bias
        dp = dot(values, head_of((qa_ref, qb_ref), head, 2 * HD), NT)
        top = jnp.max(s, axis=0, keepdims=True)
        if prev_ref is not None:
            before = prev_ref[0:1, cols]
            top = jnp.maximum(top, before)
        p = jnp.exp2((s - top) * LOG2_SCALE)
        total = jnp.sum(p, axis=0, keepdims=True)
        delta = jnp.sum(p * dp, axis=0, keepdims=True)
        if prev_ref is not None:
            fade = jnp.exp2((before - top) * LOG2_SCALE)
            total = total + prev_ref[1:2, cols] * fade
            delta = delta + prev_ref[2:3, cols] * fade
        p_ref[:, cols] = p
        dp_ref[:, cols] = dp
        stats_ref[0:1, cols] = top
        stats_ref[1:2, cols] = total
        stats_ref[2:3, cols] = delta


def grads_body(pairs, own_ref, mate_ref, qa_ref, qb_ref, *refs):
    kept, refs = refs[: 3 * pairs], refs[3 * pairs :]
    ds_refs, keep_refs, give_ref = refs[:pairs], refs[pairs : 2 * pairs], refs[2 * pairs]
    toks = qa_ref.shape[0]
    sums = [None] * pairs
    for head in range(HEADS_CHIP):
        cols = slice(head * toks, (head + 1) * toks)
        other = (head + 2) % HEADS_CHIP
        across = slice(other * toks, (other + 1) * toks)
        top_own, top_mate = own_ref[0:1, cols], mate_ref[0:1, across]
        top = jnp.maximum(top_own, top_mate)
        fade_own = jnp.exp2((top_own - top) * LOG2_SCALE)
        fade_mate = jnp.exp2((top_mate - top) * LOG2_SCALE)
        total = own_ref[1:2, cols] * fade_own + mate_ref[1:2, across] * fade_mate
        delta = own_ref[2:3, cols] * fade_own + mate_ref[2:3, across] * fade_mate
        inverse = 1.0 / total
        delta = delta * inverse
        for i in range(pairs):
            p_ref, dp_ref, stats_ref = kept[3 * i : 3 * i + 3]
            factor = jnp.exp2((stats_ref[0:1, cols] - top) * LOG2_SCALE) * inverse
            a = p_ref[:, cols] * factor
            ds = (a * (dp_ref[:, cols] - delta)).astype(BF16)
            ds_refs[i][:, cols] = ds
            dv = dot(a.astype(BF16), head_of((qa_ref, qb_ref), head, 2 * HD), NN)
            dk = dot(ds, head_of((qa_ref, qb_ref), head, 0), NN)
            if sums[i] is None:
                sums[i] = (dk, dv)
            else:
                sums[i] = (sums[i][0] + dk, sums[i][1] + dv)
    for i in range(pairs):
        both = jnp.concatenate([sums[i][0] * SCALE, sums[i][1]], axis=1)
        half = both.shape[0] // 2
        keep_refs[i][...] = both[:half]
        give_ref[i * half : (i + 1) * half, :] = both[half:].astype(BF16)


def query_body(heads, parts, *refs):
    ds_refs, refs = refs[: len(parts)], refs[len(parts) :]
    out_ref = refs[-1]
    toks = out_ref.shape[0]
    keys = []
    for count in parts:
        keys.append(joined(refs[:count])[:, :HD])
        refs = refs[count:]
    for i, head in enumerate(heads):
        dq = None
        for ds_ref, key in zip(ds_refs, keys):
            here = dot(key, ds_ref[:, head * toks : (head + 1) * toks], TN)
            dq = here if dq is None else dq + here
        out_ref[:, i * HD : (i + 1) * HD] = (jnp.transpose(dq) * SCALE).astype(out_ref.dtype)


def finish_body(*refs):
    *adds, dq_own_ref, dq_got_ref, dq_ref, dk_ref, dv_ref = refs
    dq_ref[...] = (dq_own_ref[...] + dq_got_ref[...].astype(F32)).astype(BF16)
    total = adds[0][...]
    for add in adds[1:]:
        total = total + add[...].astype(F32)
    dk_ref[...] = total[:, :HD].astype(BF16)
    dv_ref[...] = total[:, HD:].astype(BF16)


def shards(queries, key_rows, value_rows, grad_out, positions):
    toks, wide = queries.shape
    stripes = lax.axis_size("blk")
    heads = lax.axis_size("head")
    pos = positions.reshape(-1, HD)

    def route(value, offset):
        flip = 2 if offset % 2 else 0
        pairs = [
            (s * heads + h, (s + offset) % stripes * heads + (h ^ flip))
            for s in range(stripes)
            for h in range(heads)
        ]
        return lax.ppermute(value, ("blk", "head"), pairs)

    def swap(value, bit):
        return lax.ppermute(value, "head", [(h, h ^ bit) for h in range(heads)])

    def vmem(shape, dtype):
        return pltpu.VMEM(shape, dtype)

    half = toks // 2
    lanes = HEADS_CHIP * toks
    hbm = pl.BlockSpec(memory_space=pltpu.HBM)
    whole = pl.BlockSpec(memory_space=pltpu.VMEM)
    qg, kv, pos = pl.pallas_call(
        prepare,
        out_shape=[
            vmem((toks, 2 * wide), BF16),
            vmem((half, 2 * HD), BF16),
            vmem((24, HD), jnp.int32),
        ],
        in_specs=[hbm] * 5,
        out_specs=[whole] * 3,
        scratch_shapes=[pltpu.SemaphoreType.DMA((9,))],
        compiler_params=pltpu.CompilerParams(vmem_limit_bytes=16 * 1024 * 1024),
    )(*(pltpu.with_memory_space_constraint(v, pltpu.HBM) for v in (queries, grad_out, key_rows, value_rows, pos)))
    qg_mate = swap(qg, 1)
    [bias] = call(mask_body, [vmem((SPAN * half, toks), F32)], (pos,))
    window = {0: (kv,)}
    for k in (2, 1, 3):
        window[k] = (route(kv, -k),)
    kept = {}
    stats = None
    flops = 2 * 2 * HD * half * lanes
    for k in (0, 2, 1, 3):
        args = (bias, qg, qg_mate, *window[k]) + (() if stats is None else (stats,))
        p, dp, stats = call(
            lambda *refs, k=k: scores_body(k, len(window[k]), *refs),
            [vmem((half, lanes), F32), vmem((half, lanes), F32), vmem((8, lanes), F32)],
            args,
            flops=flops,
            exps=half * lanes,
        )
        kept[k] = (p, dp, stats)
    stats_mate = swap(stats, 1)
    ds = {}
    pushed = {}
    seen = stats
    for pair in ((3, 1), (2, 0)):
        outs = call(
            lambda *refs: grads_body(2, *refs),
            [vmem((half, lanes), BF16)] * 2
            + [vmem((half // 2, 2 * HD), F32)] * 2
            + [vmem((half, 2 * HD), BF16)],
            (seen, stats_mate, qg, qg_mate, *kept[pair[0]], *kept[pair[1]]),
            flops=2 * flops,
        )
        ds[pair[0]], ds[pair[1]] = outs[:2]
        keep, give = outs[2:4], outs[4]
        got = swap(give, 2)
        for i, k in enumerate(pair):
            here = got[i * half // 2 : (i + 1) * half // 2].astype(F32)
            if k:
                pushed[k] = route((keep[i] + here).astype(BF16), k)
            else:
                mine = keep[i] + here

    part = pushed[3].astype(F32) + pushed[1].astype(F32)

    def query_part(heads, kind):
        parts = [len(window[k]) for k in range(SPAN)]

        def body(*refs):
            query_body(heads, parts, *refs)

        args = [ds[k] for k in range(SPAN)] + [v for k in range(SPAN) for v in window[k]]
        return call(body, [vmem((toks, wide), kind)], args, flops=flops)[0]

    dq_got = swap(query_part((2, 3), BF16), 1)
    dq_own = query_part((0, 1), F32)
    return tuple(
        call(
            finish_body,
            [jax.ShapeDtypeStruct((toks, wide), BF16)]
            + [jax.ShapeDtypeStruct((half // 2, HD), BF16)] * 2,
            (mine, part, *(pushed[k] for k in (2,)), dq_own, dq_got),
        )
    )


def solution(mesh):
    return jax.shard_map(
        shards,
        mesh=mesh,
        in_specs=(P("blk", "head"), P("blk", None), P("blk", None), P("blk", "head"), P()),
        out_specs=(P("blk", "head"), P(("blk", "head"), None), P(("blk", "head"), None)),
        check_vma=False,
    )
```

```python
import jax
import jax.numpy as jnp
from jax import lax
from jax.experimental import pallas as pl
from jax.experimental.pallas import tpu as pltpu
from jax.sharding import PartitionSpec as P

HD = 128
SPAN = 4
HEADS_CHIP = 4
NEG = -1e30
SCALE = 1.0 / HD**0.5
LOG2_SCALE = SCALE * 1.4426950408889634
F32 = jnp.float32
BF16 = jnp.bfloat16

NT = (((1,), (1,)), ((), ()))
NN = (((1,), (0,)), ((), ()))
TN = (((0,), (0,)), ((), ()))


def dot(a, b, dims):
    return lax.dot_general(a, b, dims, preferred_element_type=F32)


def call(body, outs, args, flops=0, exps=0):
    whole = pl.BlockSpec(memory_space=pltpu.VMEM)
    return pl.pallas_call(
        body,
        out_shape=outs,
        in_specs=[whole] * len(args),
        out_specs=[whole] * len(outs),
        compiler_params=pltpu.CompilerParams(vmem_limit_bytes=16 * 1024 * 1024),
        cost_estimate=pl.CostEstimate(flops=flops, bytes_accessed=1 << 20, transcendentals=exps),
    )(*args)


def head_of(refs, head, first):
    ref = refs[head // 2]
    at = first + (head % 2) * HD
    return ref[:, at : at + HD]


def prepare(q_hbm, g_hbm, k_hbm, v_hbm, pos_hbm, qg_ref, kv_ref, pos_ref, sems):
    wide = q_hbm.shape[1]
    core = lax.axis_index("head") % 2
    chip = lax.axis_index("head") // 2
    block = lax.axis_index("blk") * (q_hbm.shape[0] // HD) // 8
    blocks = pos_hbm.shape[0] // 8
    copies = []
    for half in range(2):
        source = pl.ds(pl.multiple_of((chip ^ half) * 256 + core * 128, 128), 128)
        target = pl.ds(half * 128, 128)
        copies.append((k_hbm.at[source, :], kv_ref.at[target, pl.ds(0, HD)]))
        copies.append((v_hbm.at[source, :], kv_ref.at[target, pl.ds(HD, HD)]))
    copies.append((q_hbm, qg_ref.at[:, pl.ds(0, wide)]))
    copies.append((g_hbm, qg_ref.at[:, pl.ds(wide, wide)]))
    for i in range(3):
        row = pl.multiple_of((block + i) % blocks * 8, 8)
        copies.append((pos_hbm.at[pl.ds(row, 8), :], pos_ref.at[pl.ds(i * 8, 8), :]))
    copies = [
        pltpu.make_async_copy(source, target, sems.at[i])
        for i, (source, target) in enumerate(copies)
    ]
    for copy in copies:
        copy.start()
    for copy in copies:
        copy.wait()


def mask_body(pos_ref, bias_ref):
    core = lax.axis_index("head") % 2
    chip = lax.axis_index("head") // 2
    toks = bias_ref.shape[1]
    query_row = lax.axis_index("blk") * (toks // HD) % 8
    queries = [
        pos_ref[pl.ds(query_row + i, 1), :].astype(F32) for i in range(toks // HD)
    ]
    for k in range(SPAN):
        for half in range(2):
            place = query_row + k * (toks // HD) + 2 * (chip ^ (k + half) % 2) + core
            row = pos_ref[pl.ds(place, 1), :]
            keys = jnp.transpose(jnp.broadcast_to(row.astype(F32), (HD, HD)))
            rows = slice((2 * k + half) * HD, (2 * k + half + 1) * HD)
            for i, query in enumerate(queries):
                bias_ref[rows, i * HD : (i + 1) * HD] = jnp.where(keys <= query, 0.0, NEG)


def joined(refs):
    return refs[0][...] if len(refs) == 1 else jnp.concatenate([r[...] for r in refs], axis=0)


def scores_body(offset, parts, bias_ref, qa_ref, qb_ref, *refs):
    kv, refs = joined(refs[:parts]), refs[parts:]
    prev_ref = refs[0] if len(refs) == 4 else None
    p_ref, dp_ref, stats_ref = refs[-3:]
    rows = kv.shape[0]
    toks = qa_ref.shape[0]
    bias = bias_ref[offset * rows : (offset + 1) * rows, :]
    keys = kv[:, :HD]
    values = kv[:, HD:]
    for head in range(HEADS_CHIP):
        cols = slice(head * toks, (head + 1) * toks)
        s = dot(keys, head_of((qa_ref, qb_ref), head, 0), NT) + bias
        dp = dot(values, head_of((qa_ref, qb_ref), head, 2 * HD), NT)
        top = jnp.max(s, axis=0, keepdims=True)
        if prev_ref is not None:
            before = prev_ref[0:1, cols]
            top = jnp.maximum(top, before)
        p = jnp.exp2((s - top) * LOG2_SCALE)
        total = jnp.sum(p, axis=0, keepdims=True)
        delta = jnp.sum(p * dp, axis=0, keepdims=True)
        if prev_ref is not None:
            fade = jnp.exp2((before - top) * LOG2_SCALE)
            total = total + prev_ref[1:2, cols] * fade
            delta = delta + prev_ref[2:3, cols] * fade
        p_ref[:, cols] = p
        dp_ref[:, cols] = dp
        stats_ref[0:1, cols] = top
        stats_ref[1:2, cols] = total
        stats_ref[2:3, cols] = delta


def grads_body(pairs, own_ref, mate_ref, qa_ref, qb_ref, *refs):
    kept, refs = refs[: 3 * pairs], refs[3 * pairs :]
    ds_refs, keep_refs, give_ref = refs[:pairs], refs[pairs : 2 * pairs], refs[2 * pairs]
    toks = qa_ref.shape[0]
    sums = [None] * pairs
    for head in range(HEADS_CHIP):
        cols = slice(head * toks, (head + 1) * toks)
        other = (head + 2) % HEADS_CHIP
        across = slice(other * toks, (other + 1) * toks)
        top_own, top_mate = own_ref[0:1, cols], mate_ref[0:1, across]
        top = jnp.maximum(top_own, top_mate)
        fade_own = jnp.exp2((top_own - top) * LOG2_SCALE)
        fade_mate = jnp.exp2((top_mate - top) * LOG2_SCALE)
        total = own_ref[1:2, cols] * fade_own + mate_ref[1:2, across] * fade_mate
        delta = own_ref[2:3, cols] * fade_own + mate_ref[2:3, across] * fade_mate
        inverse = 1.0 / total
        delta = delta * inverse
        for i in range(pairs):
            p_ref, dp_ref, stats_ref = kept[3 * i : 3 * i + 3]
            factor = jnp.exp2((stats_ref[0:1, cols] - top) * LOG2_SCALE) * inverse
            a = p_ref[:, cols] * factor
            ds = (a * (dp_ref[:, cols] - delta)).astype(BF16)
            ds_refs[i][:, cols] = ds
            dv = dot(a.astype(BF16), head_of((qa_ref, qb_ref), head, 2 * HD), NN)
            dk = dot(ds, head_of((qa_ref, qb_ref), head, 0), NN)
            if sums[i] is None:
                sums[i] = (dk, dv)
            else:
                sums[i] = (sums[i][0] + dk, sums[i][1] + dv)
    for i in range(pairs):
        both = jnp.concatenate([sums[i][0] * SCALE, sums[i][1]], axis=1)
        half = both.shape[0] // 2
        keep_refs[i][...] = both[:half]
        give_ref[i * half : (i + 1) * half, :] = both[half:].astype(BF16)


def query_body(heads, parts, *refs):
    ds_refs, refs = refs[: len(parts)], refs[len(parts) :]
    out_ref = refs[-1]
    toks = out_ref.shape[0]
    keys = []
    for count in parts:
        keys.append(joined(refs[:count])[:, :HD])
        refs = refs[count:]
    for i, head in enumerate(heads):
        dq = None
        for ds_ref, key in zip(ds_refs, keys):
            here = dot(key, ds_ref[:, head * toks : (head + 1) * toks], TN)
            dq = here if dq is None else dq + here
        out_ref[:, i * HD : (i + 1) * HD] = (jnp.transpose(dq) * SCALE).astype(out_ref.dtype)


def finish_body(*refs):
    *adds, dq_own_ref, dq_got_ref, dq_ref, dk_ref, dv_ref = refs
    dq_ref[...] = (dq_own_ref[...] + dq_got_ref[...].astype(F32)).astype(BF16)
    total = adds[0][...]
    for add in adds[1:]:
        total = total + add[...].astype(F32)
    dk_ref[...] = total[:, :HD].astype(BF16)
    dv_ref[...] = total[:, HD:].astype(BF16)


def shards(queries, key_rows, value_rows, grad_out, positions):
    toks, wide = queries.shape
    stripes = lax.axis_size("blk")
    heads = lax.axis_size("head")
    pos = positions.reshape(-1, HD)

    def route(value, offset):
        flip = 2 if offset % 2 else 0
        pairs = [
            (s * heads + h, (s + offset) % stripes * heads + (h ^ flip))
            for s in range(stripes)
            for h in range(heads)
        ]
        return lax.ppermute(value, ("blk", "head"), pairs)

    def swap(value, bit):
        return lax.ppermute(value, "head", [(h, h ^ bit) for h in range(heads)])

    def vmem(shape, dtype):
        return pltpu.VMEM(shape, dtype)

    half = toks // 2
    lanes = HEADS_CHIP * toks
    hbm = pl.BlockSpec(memory_space=pltpu.HBM)
    whole = pl.BlockSpec(memory_space=pltpu.VMEM)
    qg, kv, pos = pl.pallas_call(
        prepare,
        out_shape=[
            vmem((toks, 2 * wide), BF16),
            vmem((half, 2 * HD), BF16),
            vmem((24, HD), jnp.int32),
        ],
        in_specs=[hbm] * 5,
        out_specs=[whole] * 3,
        scratch_shapes=[pltpu.SemaphoreType.DMA((9,))],
        compiler_params=pltpu.CompilerParams(vmem_limit_bytes=16 * 1024 * 1024),
    )(*(pltpu.with_memory_space_constraint(v, pltpu.HBM) for v in (queries, grad_out, key_rows, value_rows, pos)))
    qg_mate = swap(qg, 1)
    [bias] = call(mask_body, [vmem((SPAN * half, toks), F32)], (pos,))
    window = {0: (kv,)}
    for k in (2, 1, 3):
        window[k] = (route(kv, -k),)
    kept = {}
    stats = None
    flops = 2 * 2 * HD * half * lanes
    for k in (0, 2, 1, 3):
        args = (bias, qg, qg_mate, *window[k]) + (() if stats is None else (stats,))
        p, dp, stats = call(
            lambda *refs, k=k: scores_body(k, len(window[k]), *refs),
            [vmem((half, lanes), F32), vmem((half, lanes), F32), vmem((8, lanes), F32)],
            args,
            flops=flops,
            exps=half * lanes,
        )
        kept[k] = (p, dp, stats)
    stats_mate = swap(stats, 1)
    ds = {}
    pushed = {}
    quarter = half // 2
    ready = {}
    gives = []
    seen = stats
    for group in ((3,), (2, 1), (0,)):
        count = len(group)
        outs = call(
            lambda *refs, count=count: grads_body(count, *refs),
            [vmem((half, lanes), BF16)] * count
            + [vmem((quarter, 2 * HD), F32)] * count
            + [vmem((count * quarter, 2 * HD), BF16)],
            (seen, stats_mate, qg, qg_mate, *(v for k in group for v in kept[k])),
            flops=count * flops,
        )
        for i, k in enumerate(group):
            ds[k] = outs[i]
        keep, give = outs[count : 2 * count], outs[2 * count]
        gives.append(give)
        got = swap(give, 2)
        for i, k in enumerate(group):
            total = keep[i] + got[i * quarter : (i + 1) * quarter].astype(F32)
            if k:
                ready[k] = total.astype(BF16)
                pushed[k] = route(ready[k], k)
            else:
                mine = total
        seen, *_ = lax.optimization_barrier((stats, give, *([ready[3]] if len(gives) == 2 else [])))

    part = pushed[3].astype(F32) + pushed[1].astype(F32) + pushed[2].astype(F32)

    def query_part(heads, kind):
        parts = [len(window[k]) for k in range(SPAN)]

        def body(*refs):
            query_body(heads, parts, *refs)

        args = [ds[k] for k in range(SPAN)] + [v for k in range(SPAN) for v in window[k]]
        return call(body, [vmem((toks, wide), kind)], args, flops=flops)[0]

    dq_got = swap(query_part((2, 3), BF16), 1)
    dq_own = query_part((0, 1), F32)
    return tuple(
        call(
            finish_body,
            [jax.ShapeDtypeStruct((toks, wide), BF16)]
            + [jax.ShapeDtypeStruct((half // 2, HD), BF16)] * 2,
            (mine, part, dq_own, dq_got),
        )
    )


def solution(mesh):
    return jax.shard_map(
        shards,
        mesh=mesh,
        in_specs=(P("blk", "head"), P("blk", None), P("blk", None), P("blk", "head"), P()),
        out_specs=(P("blk", "head"), P(("blk", "head"), None), P(("blk", "head"), None)),
        check_vma=False,
    )
```

```python
import jax
import jax.numpy as jnp
from jax import lax
from jax.experimental import pallas as pl
from jax.experimental.pallas import tpu as pltpu
from jax.sharding import PartitionSpec as P

HD = 128
SPAN = 4
HEADS_CHIP = 4
NEG = -1e30
SCALE = 1.0 / HD**0.5
LOG2_SCALE = SCALE * 1.4426950408889634
F32 = jnp.float32
BF16 = jnp.bfloat16

NT = (((1,), (1,)), ((), ()))
NN = (((1,), (0,)), ((), ()))
TN = (((0,), (0,)), ((), ()))


def dot(a, b, dims):
    return lax.dot_general(a, b, dims, preferred_element_type=F32)


def call(body, outs, args, flops=0, exps=0):
    whole = pl.BlockSpec(memory_space=pltpu.VMEM)
    return pl.pallas_call(
        body,
        out_shape=outs,
        in_specs=[whole] * len(args),
        out_specs=[whole] * len(outs),
        compiler_params=pltpu.CompilerParams(vmem_limit_bytes=16 * 1024 * 1024),
        cost_estimate=pl.CostEstimate(flops=flops, bytes_accessed=1 << 20, transcendentals=exps),
    )(*args)


def head_of(refs, head, first):
    ref = refs[head // 2]
    at = first + (head % 2) * HD
    return ref[:, at : at + HD]


def prepare(q_hbm, g_hbm, k_hbm, v_hbm, pos_hbm, qg_ref, kv_ref, pos_ref, sems):
    wide = q_hbm.shape[1]
    core = lax.axis_index("head") % 2
    chip = lax.axis_index("head") // 2
    block = lax.axis_index("blk") * (q_hbm.shape[0] // HD) // 8
    blocks = pos_hbm.shape[0] // 8
    copies = []
    for half in range(2):
        source = pl.ds(pl.multiple_of((chip ^ half) * 256 + core * 128, 128), 128)
        target = pl.ds(half * 128, 128)
        copies.append((k_hbm.at[source, :], kv_ref.at[target, pl.ds(0, HD)]))
        copies.append((v_hbm.at[source, :], kv_ref.at[target, pl.ds(HD, HD)]))
    copies.append((q_hbm, qg_ref.at[:, pl.ds(0, wide)]))
    copies.append((g_hbm, qg_ref.at[:, pl.ds(wide, wide)]))
    for i in range(3):
        row = pl.multiple_of((block + i) % blocks * 8, 8)
        copies.append((pos_hbm.at[pl.ds(row, 8), :], pos_ref.at[pl.ds(i * 8, 8), :]))
    copies = [
        pltpu.make_async_copy(source, target, sems.at[i])
        for i, (source, target) in enumerate(copies)
    ]
    for copy in copies:
        copy.start()
    for copy in copies:
        copy.wait()


def mask_body(pos_ref, bias_ref):
    core = lax.axis_index("head") % 2
    chip = lax.axis_index("head") // 2
    toks = bias_ref.shape[1]
    query_row = lax.axis_index("blk") * (toks // HD) % 8
    queries = [
        pos_ref[pl.ds(query_row + i, 1), :].astype(F32) for i in range(toks // HD)
    ]
    for k in range(SPAN):
        for half in range(2):
            place = query_row + k * (toks // HD) + 2 * (chip ^ (k + half) % 2) + core
            row = pos_ref[pl.ds(place, 1), :]
            keys = jnp.transpose(jnp.broadcast_to(row.astype(F32), (HD, HD)))
            rows = slice((2 * k + half) * HD, (2 * k + half + 1) * HD)
            for i, query in enumerate(queries):
                bias_ref[rows, i * HD : (i + 1) * HD] = jnp.where(keys <= query, 0.0, NEG)


def joined(refs):
    return refs[0][...] if len(refs) == 1 else jnp.concatenate([r[...] for r in refs], axis=0)


def scores_body(offset, parts, bias_ref, qa_ref, qb_ref, *refs):
    kv, refs = joined(refs[:parts]), refs[parts:]
    prev_ref = refs[0] if len(refs) == 4 else None
    p_ref, dp_ref, stats_ref = refs[-3:]
    rows = kv.shape[0]
    toks = qa_ref.shape[0]
    bias = bias_ref[offset * rows : (offset + 1) * rows, :]
    keys = kv[:, :HD]
    values = kv[:, HD:]
    for head in range(HEADS_CHIP):
        cols = slice(head * toks, (head + 1) * toks)
        s = dot(keys, head_of((qa_ref, qb_ref), head, 0), NT) + bias
        dp = dot(values, head_of((qa_ref, qb_ref), head, 2 * HD), NT)
        top = jnp.max(s, axis=0, keepdims=True)
        if prev_ref is not None:
            before = prev_ref[0:1, cols]
            top = jnp.maximum(top, before)
        p = jnp.exp2((s - top) * LOG2_SCALE)
        total = jnp.sum(p, axis=0, keepdims=True)
        delta = jnp.sum(p * dp, axis=0, keepdims=True)
        if prev_ref is not None:
            fade = jnp.exp2((before - top) * LOG2_SCALE)
            total = total + prev_ref[1:2, cols] * fade
            delta = delta + prev_ref[2:3, cols] * fade
        p_ref[:, cols] = p
        dp_ref[:, cols] = dp
        stats_ref[0:1, cols] = top
        stats_ref[1:2, cols] = total
        stats_ref[2:3, cols] = delta


def grads_body(pairs, split, own_ref, mate_ref, qa_ref, qb_ref, *refs):
    kept, refs = refs[: 3 * pairs], refs[3 * pairs :]
    ds_refs, outs = refs[:pairs], refs[pairs:]
    toks = qa_ref.shape[0]
    sums = [None] * pairs
    for head in range(HEADS_CHIP):
        cols = slice(head * toks, (head + 1) * toks)
        other = (head + 2) % HEADS_CHIP
        across = slice(other * toks, (other + 1) * toks)
        top_own, top_mate = own_ref[0:1, cols], mate_ref[0:1, across]
        top = jnp.maximum(top_own, top_mate)
        fade_own = jnp.exp2((top_own - top) * LOG2_SCALE)
        fade_mate = jnp.exp2((top_mate - top) * LOG2_SCALE)
        total = own_ref[1:2, cols] * fade_own + mate_ref[1:2, across] * fade_mate
        delta = own_ref[2:3, cols] * fade_own + mate_ref[2:3, across] * fade_mate
        inverse = 1.0 / total
        delta = delta * inverse
        for i in range(pairs):
            p_ref, dp_ref, stats_ref = kept[3 * i : 3 * i + 3]
            factor = jnp.exp2((stats_ref[0:1, cols] - top) * LOG2_SCALE) * inverse
            a = p_ref[:, cols] * factor
            ds = (a * (dp_ref[:, cols] - delta)).astype(BF16)
            ds_refs[i][:, cols] = ds
            dv = dot(a.astype(BF16), head_of((qa_ref, qb_ref), head, 2 * HD), NN)
            dk = dot(ds, head_of((qa_ref, qb_ref), head, 0), NN)
            if sums[i] is None:
                sums[i] = (dk, dv)
            else:
                sums[i] = (sums[i][0] + dk, sums[i][1] + dv)
    for i in range(pairs):
        both = jnp.concatenate([sums[i][0] * SCALE, sums[i][1]], axis=1)
        half = both.shape[0] // 2
        if split:
            outs[i][...] = both[:half]
            outs[pairs][i * half : (i + 1) * half, :] = both[half:].astype(BF16)
        else:
            outs[i][...] = both.astype(outs[i].dtype)


def query_body(heads, parts, *refs):
    ds_refs, refs = refs[: len(parts)], refs[len(parts) :]
    out_ref = refs[-1]
    toks = out_ref.shape[0]
    keys = []
    for count in parts:
        keys.append(joined(refs[:count])[:, :HD])
        refs = refs[count:]
    for i, head in enumerate(heads):
        dq = None
        for ds_ref, key in zip(ds_refs, keys):
            here = dot(key, ds_ref[:, head * toks : (head + 1) * toks], TN)
            dq = here if dq is None else dq + here
        out_ref[:, i * HD : (i + 1) * HD] = (jnp.transpose(dq) * SCALE).astype(out_ref.dtype)


def finish_body(*refs):
    *adds, dq_own_ref, dq_got_ref, dq_ref, dk_ref, dv_ref = refs
    dq_ref[...] = (dq_own_ref[...] + dq_got_ref[...].astype(F32)).astype(BF16)
    total = adds[0][...]
    for add in adds[1:]:
        total = total + add[...].astype(F32)
    dk_ref[...] = total[:, :HD].astype(BF16)
    dv_ref[...] = total[:, HD:].astype(BF16)


def shards(queries, key_rows, value_rows, grad_out, positions):
    toks, wide = queries.shape
    stripes = lax.axis_size("blk")
    heads = lax.axis_size("head")
    pos = positions.reshape(-1, HD)

    def route(value, offset):
        flip = 2 if offset % 2 else 0
        pairs = [
            (s * heads + h, (s + offset) % stripes * heads + (h ^ flip))
            for s in range(stripes)
            for h in range(heads)
        ]
        return lax.ppermute(value, ("blk", "head"), pairs)

    def swap(value, bit):
        return lax.ppermute(value, "head", [(h, h ^ bit) for h in range(heads)])

    def vmem(shape, dtype):
        return pltpu.VMEM(shape, dtype)

    half = toks // 2
    lanes = HEADS_CHIP * toks
    hbm = pl.BlockSpec(memory_space=pltpu.HBM)
    whole = pl.BlockSpec(memory_space=pltpu.VMEM)
    qg, kv, pos = pl.pallas_call(
        prepare,
        out_shape=[
            vmem((toks, 2 * wide), BF16),
            vmem((half, 2 * HD), BF16),
            vmem((24, HD), jnp.int32),
        ],
        in_specs=[hbm] * 5,
        out_specs=[whole] * 3,
        scratch_shapes=[pltpu.SemaphoreType.DMA((9,))],
        compiler_params=pltpu.CompilerParams(vmem_limit_bytes=16 * 1024 * 1024),
    )(*(pltpu.with_memory_space_constraint(v, pltpu.HBM) for v in (queries, grad_out, key_rows, value_rows, pos)))
    qg_mate = swap(qg, 1)
    [bias] = call(mask_body, [vmem((SPAN * half, toks), F32)], (pos,))
    window = {0: (kv,)}
    for k in (2, 1, 3):
        window[k] = (route(kv, -k),)
    kept = {}
    stats = None
    flops = 2 * 2 * HD * half * lanes
    for k in (0, 2, 1, 3):
        args = (bias, qg, qg_mate, *window[k]) + (() if stats is None else (stats,))
        p, dp, stats = call(
            lambda *refs, k=k: scores_body(k, len(window[k]), *refs),
            [vmem((half, lanes), F32), vmem((half, lanes), F32), vmem((8, lanes), F32)],
            args,
            flops=flops,
            exps=half * lanes,
        )
        kept[k] = (p, dp, stats)
    stats_mate = swap(stats, 1)
    ds = {}
    quarter = half // 2

    def grads(ks, split, outs, seen):
        got = call(
            lambda *refs: grads_body(len(ks), split, *refs),
            [vmem((half, lanes), BF16)] * len(ks) + outs,
            (seen, stats_mate, qg, qg_mate, *(v for k in ks for v in kept[k])),
            flops=len(ks) * flops,
        )
        for k, value in zip(ks, got):
            ds[k] = value
        return got[len(ks) :]

    keep3, keep2, give = grads(
        (3, 2),
        True,
        [vmem((quarter, 2 * HD), F32)] * 2 + [vmem((half, 2 * HD), BF16)],
        stats,
    )
    got = swap(give, 2)
    seen, _ = lax.optimization_barrier((stats, give))
    [one] = grads((1,), False, [vmem((half, 2 * HD), BF16)], seen)
    one_got = route(one, 1)
    seen, _ = lax.optimization_barrier((stats, one))
    [zero] = grads((0,), False, [vmem((half, 2 * HD), F32)], seen)
    low3 = (keep3 + got[:quarter].astype(F32)).astype(BF16)
    low2 = (keep2 + got[quarter:].astype(F32)).astype(BF16)
    pushed = [route(low3, 3), route(low2, 2)]
    one_got, *_ = lax.optimization_barrier((one_got, low3, low2))
    mine = zero[:quarter] + one_got[:quarter].astype(F32)
    mine_got = swap((zero[quarter:] + one_got[quarter:].astype(F32)).astype(BF16), 2)

    part = pushed[0].astype(F32) + pushed[1].astype(F32)

    def query_part(heads, kind):
        parts = [len(window[k]) for k in range(SPAN)]

        def body(*refs):
            query_body(heads, parts, *refs)

        args = [ds[k] for k in range(SPAN)] + [v for k in range(SPAN) for v in window[k]]
        return call(body, [vmem((toks, wide), kind)], args, flops=flops)[0]

    dq_got = swap(query_part((2, 3), BF16), 1)
    dq_own = query_part((0, 1), F32)
    return tuple(
        call(
            finish_body,
            [jax.ShapeDtypeStruct((toks, wide), BF16)]
            + [jax.ShapeDtypeStruct((half // 2, HD), BF16)] * 2,
            (mine, mine_got, part, dq_own, dq_got),
        )
    )


def solution(mesh):
    return jax.shard_map(
        shards,
        mesh=mesh,
        in_specs=(P("blk", "head"), P("blk", None), P("blk", None), P("blk", "head"), P()),
        out_specs=(P("blk", "head"), P(("blk", "head"), None), P(("blk", "head"), None)),
        check_vma=False,
    )
```

```python
import jax
import jax.numpy as jnp
from jax import lax
from jax.experimental import pallas as pl
from jax.experimental.pallas import tpu as pltpu
from jax.sharding import PartitionSpec as P

HD = 128
SPAN = 4
HEADS_CHIP = 4
NEG = -1e30
SCALE = 1.0 / HD**0.5
LOG2_SCALE = SCALE * 1.4426950408889634
F32 = jnp.float32
BF16 = jnp.bfloat16

NT = (((1,), (1,)), ((), ()))
NN = (((1,), (0,)), ((), ()))
TN = (((0,), (0,)), ((), ()))


def dot(a, b, dims):
    return lax.dot_general(a, b, dims, preferred_element_type=F32)


def call(body, outs, args, flops=0, exps=0):
    whole = pl.BlockSpec(memory_space=pltpu.VMEM)
    return pl.pallas_call(
        body,
        out_shape=outs,
        in_specs=[whole] * len(args),
        out_specs=[whole] * len(outs),
        compiler_params=pltpu.CompilerParams(vmem_limit_bytes=16 * 1024 * 1024),
        cost_estimate=pl.CostEstimate(flops=flops, bytes_accessed=1 << 20, transcendentals=exps),
    )(*args)


def head_of(refs, head, first):
    ref = refs[head // 2]
    at = first + (head % 2) * HD
    return ref[:, at : at + HD]


def prepare(q_hbm, g_hbm, k_hbm, v_hbm, qg_ref, kv_ref, sems):
    wide = q_hbm.shape[1]
    core = lax.axis_index("head") % 2
    chip = lax.axis_index("head") // 2
    copies = []
    for half in range(2):
        source = pl.ds(pl.multiple_of((chip ^ half) * 256 + core * 128, 128), 128)
        target = pl.ds(half * 128, 128)
        copies.append((k_hbm.at[source, :], kv_ref.at[target, pl.ds(0, HD)]))
        copies.append((v_hbm.at[source, :], kv_ref.at[target, pl.ds(HD, HD)]))
    copies.append((q_hbm, qg_ref.at[:, pl.ds(0, wide)]))
    copies.append((g_hbm, qg_ref.at[:, pl.ds(wide, wide)]))
    copies = [
        pltpu.make_async_copy(source, target, sems.at[i])
        for i, (source, target) in enumerate(copies)
    ]
    for copy in copies:
        copy.start()
    for copy in copies:
        copy.wait()


def mask_body(pos_hbm, bias_ref, pos_ref, sems):
    block = lax.axis_index("blk") * (bias_ref.shape[1] // HD) // 8
    blocks = pos_hbm.shape[0] // 8
    copies = []
    for i in range(3):
        row = pl.multiple_of((block + i) % blocks * 8, 8)
        source, target = pos_hbm.at[pl.ds(row, 8), :], pos_ref.at[pl.ds(i * 8, 8), :]
        copies.append(pltpu.make_async_copy(source, target, sems.at[i]))
    for copy in copies:
        copy.start()
    for copy in copies:
        copy.wait()
    core = lax.axis_index("head") % 2
    chip = lax.axis_index("head") // 2
    toks = bias_ref.shape[1]
    query_row = lax.axis_index("blk") * (toks // HD) % 8
    queries = [
        pos_ref[pl.ds(query_row + i, 1), :].astype(F32) for i in range(toks // HD)
    ]
    for k in range(SPAN):
        for half in range(2):
            place = query_row + k * (toks // HD) + 2 * (chip ^ (k + half) % 2) + core
            row = pos_ref[pl.ds(place, 1), :]
            keys = jnp.transpose(jnp.broadcast_to(row.astype(F32), (HD, HD)))
            rows = slice((2 * k + half) * HD, (2 * k + half + 1) * HD)
            for i, query in enumerate(queries):
                bias_ref[rows, i * HD : (i + 1) * HD] = jnp.where(keys <= query, 0.0, NEG)


def joined(refs):
    return refs[0][...] if len(refs) == 1 else jnp.concatenate([r[...] for r in refs], axis=0)


def scores_body(offset, parts, bias_ref, qa_ref, qb_ref, *refs):
    kv, refs = joined(refs[:parts]), refs[parts:]
    prev_ref = refs[0] if len(refs) == 4 else None
    p_ref, dp_ref, stats_ref = refs[-3:]
    rows = kv.shape[0]
    toks = qa_ref.shape[0]
    bias = bias_ref[offset * rows : (offset + 1) * rows, :]
    keys = kv[:, :HD]
    values = kv[:, HD:]
    for head in range(HEADS_CHIP):
        cols = slice(head * toks, (head + 1) * toks)
        s = dot(keys, head_of((qa_ref, qb_ref), head, 0), NT) + bias
        dp = dot(values, head_of((qa_ref, qb_ref), head, 2 * HD), NT)
        top = jnp.max(s, axis=0, keepdims=True)
        if prev_ref is not None:
            before = prev_ref[0:1, cols]
            top = jnp.maximum(top, before)
        p = jnp.exp2((s - top) * LOG2_SCALE)
        total = jnp.sum(p, axis=0, keepdims=True)
        delta = jnp.sum(p * dp, axis=0, keepdims=True)
        if prev_ref is not None:
            fade = jnp.exp2((before - top) * LOG2_SCALE)
            total = total + prev_ref[1:2, cols] * fade
            delta = delta + prev_ref[2:3, cols] * fade
        p_ref[:, cols] = p
        dp_ref[:, cols] = dp
        stats_ref[0:1, cols] = top
        stats_ref[1:2, cols] = total
        stats_ref[2:3, cols] = delta


def grads_body(pairs, own_ref, mate_ref, qa_ref, qb_ref, *refs):
    kept, refs = refs[: 3 * pairs], refs[3 * pairs :]
    ds_refs, keep_refs, give_ref = refs[:pairs], refs[pairs : 2 * pairs], refs[2 * pairs]
    toks = qa_ref.shape[0]
    sums = [None] * pairs
    for head in range(HEADS_CHIP):
        cols = slice(head * toks, (head + 1) * toks)
        other = (head + 2) % HEADS_CHIP
        across = slice(other * toks, (other + 1) * toks)
        top_own, top_mate = own_ref[0:1, cols], mate_ref[0:1, across]
        top = jnp.maximum(top_own, top_mate)
        fade_own = jnp.exp2((top_own - top) * LOG2_SCALE)
        fade_mate = jnp.exp2((top_mate - top) * LOG2_SCALE)
        total = own_ref[1:2, cols] * fade_own + mate_ref[1:2, across] * fade_mate
        delta = own_ref[2:3, cols] * fade_own + mate_ref[2:3, across] * fade_mate
        inverse = 1.0 / total
        delta = delta * inverse
        for i in range(pairs):
            p_ref, dp_ref, stats_ref = kept[3 * i : 3 * i + 3]
            factor = jnp.exp2((stats_ref[0:1, cols] - top) * LOG2_SCALE) * inverse
            a = p_ref[:, cols] * factor
            ds = (a * (dp_ref[:, cols] - delta)).astype(BF16)
            ds_refs[i][:, cols] = ds
            dv = dot(a.astype(BF16), head_of((qa_ref, qb_ref), head, 2 * HD), NN)
            dk = dot(ds, head_of((qa_ref, qb_ref), head, 0), NN)
            if sums[i] is None:
                sums[i] = (dk, dv)
            else:
                sums[i] = (sums[i][0] + dk, sums[i][1] + dv)
    for i in range(pairs):
        both = jnp.concatenate([sums[i][0] * SCALE, sums[i][1]], axis=1)
        half = both.shape[0] // 2
        keep_refs[i][...] = both[:half]
        give_ref[i * half : (i + 1) * half, :] = both[half:].astype(BF16)


def query_body(heads, parts, *refs):
    ds_refs, refs = refs[: len(parts)], refs[len(parts) :]
    out_ref = refs[-1]
    toks = out_ref.shape[0]
    keys = []
    for count in parts:
        keys.append(joined(refs[:count])[:, :HD])
        refs = refs[count:]
    for i, head in enumerate(heads):
        dq = None
        for ds_ref, key in zip(ds_refs, keys):
            here = dot(key, ds_ref[:, head * toks : (head + 1) * toks], TN)
            dq = here if dq is None else dq + here
        out_ref[:, i * HD : (i + 1) * HD] = (jnp.transpose(dq) * SCALE).astype(out_ref.dtype)


def finish_body(*refs):
    *adds, dq_own_ref, dq_got_ref, dq_ref, dk_ref, dv_ref = refs
    dq_ref[...] = (dq_own_ref[...] + dq_got_ref[...].astype(F32)).astype(BF16)
    total = adds[0][...]
    for add in adds[1:]:
        total = total + add[...].astype(F32)
    dk_ref[...] = total[:, :HD].astype(BF16)
    dv_ref[...] = total[:, HD:].astype(BF16)


def shards(queries, key_rows, value_rows, grad_out, positions):
    toks, wide = queries.shape
    stripes = lax.axis_size("blk")
    heads = lax.axis_size("head")
    pos = positions.reshape(-1, HD)

    def route(value, offset):
        flip = 2 if offset % 2 else 0
        pairs = [
            (s * heads + h, (s + offset) % stripes * heads + (h ^ flip))
            for s in range(stripes)
            for h in range(heads)
        ]
        return lax.ppermute(value, ("blk", "head"), pairs)

    def swap(value, bit):
        return lax.ppermute(value, "head", [(h, h ^ bit) for h in range(heads)])

    def vmem(shape, dtype):
        return pltpu.VMEM(shape, dtype)

    half = toks // 2
    lanes = HEADS_CHIP * toks
    hbm = pl.BlockSpec(memory_space=pltpu.HBM)
    whole = pl.BlockSpec(memory_space=pltpu.VMEM)
    def fetch(body, outs, scratch, inputs):
        return pl.pallas_call(
            body,
            out_shape=outs,
            in_specs=[hbm] * len(inputs),
            out_specs=[whole] * len(outs),
            scratch_shapes=scratch,
            compiler_params=pltpu.CompilerParams(vmem_limit_bytes=16 * 1024 * 1024),
        )(*(pltpu.with_memory_space_constraint(v, pltpu.HBM) for v in inputs))

    qg, kv = fetch(
        prepare,
        [vmem((toks, 2 * wide), BF16), vmem((half, 2 * HD), BF16)],
        [pltpu.SemaphoreType.DMA((6,))],
        (queries, grad_out, key_rows, value_rows),
    )
    qg_mate = swap(qg, 1)
    [bias] = fetch(
        mask_body,
        [vmem((SPAN * half, toks), F32)],
        [pltpu.VMEM((24, HD), jnp.int32), pltpu.SemaphoreType.DMA((3,))],
        (pos,),
    )
    window = {0: (kv,)}
    for k in (2, 1, 3):
        window[k] = (route(kv, -k),)
    kept = {}
    stats = None
    flops = 2 * 2 * HD * half * lanes
    for k in (0, 2, 1, 3):
        args = (bias, qg, qg_mate, *window[k]) + (() if stats is None else (stats,))
        p, dp, stats = call(
            lambda *refs, k=k: scores_body(k, len(window[k]), *refs),
            [vmem((half, lanes), F32), vmem((half, lanes), F32), vmem((8, lanes), F32)],
            args,
            flops=flops,
            exps=half * lanes,
        )
        kept[k] = (p, dp, stats)
    stats_mate = swap(stats, 1)
    ds = {}
    pushed = {}
    quarter = half // 2
    ready = {}
    gives = []
    seen = stats
    for group in ((3,), (2, 1), (0,)):
        count = len(group)
        outs = call(
            lambda *refs, count=count: grads_body(count, *refs),
            [vmem((half, lanes), BF16)] * count
            + [vmem((quarter, 2 * HD), F32)] * count
            + [vmem((count * quarter, 2 * HD), BF16)],
            (seen, stats_mate, qg, qg_mate, *(v for k in group for v in kept[k])),
            flops=count * flops,
        )
        for i, k in enumerate(group):
            ds[k] = outs[i]
        keep, give = outs[count : 2 * count], outs[2 * count]
        gives.append(give)
        got = swap(give, 2)
        for i, k in enumerate(group):
            total = keep[i] + got[i * quarter : (i + 1) * quarter].astype(F32)
            if k:
                ready[k] = total.astype(BF16)
                pushed[k] = route(ready[k], k)
            else:
                mine = total
        seen, *_ = lax.optimization_barrier((stats, give, *([ready[3]] if len(gives) == 2 else [])))

    part = pushed[3].astype(F32) + pushed[1].astype(F32) + pushed[2].astype(F32)

    def query_part(heads, kind):
        parts = [len(window[k]) for k in range(SPAN)]

        def body(*refs):
            query_body(heads, parts, *refs)

        args = [ds[k] for k in range(SPAN)] + [v for k in range(SPAN) for v in window[k]]
        return call(body, [vmem((toks, wide), kind)], args, flops=flops)[0]

    dq_got = swap(query_part((2, 3), BF16), 1)
    dq_own = query_part((0, 1), F32)
    return tuple(
        call(
            finish_body,
            [jax.ShapeDtypeStruct((toks, wide), BF16)]
            + [jax.ShapeDtypeStruct((half // 2, HD), BF16)] * 2,
            (mine, part, dq_own, dq_got),
        )
    )


def solution(mesh):
    return jax.shard_map(
        shards,
        mesh=mesh,
        in_specs=(P("blk", "head"), P("blk", None), P("blk", None), P("blk", "head"), P()),
        out_specs=(P("blk", "head"), P(("blk", "head"), None), P(("blk", "head"), None)),
        check_vma=False,
    )
```
